32 devices in a mesh: prow: 16 (over z, y, core), pcol: 2 (over x).
Axes of the slice: x: 2, y: 2, z: 4, core: 2. Of those that a mesh axis runs over, the one named last changes fastest.
Arguments:
- inverse: float32 [2048, 2048], P('prow', 'pcol'), may hold values from -12 to 12, as said below
- factor_one: bfloat16 [2048, 512], P('prow'), may hold values from -0.1875 to 0.1875
- factor_two: bfloat16 [2048, 512], P('prow'), may hold values from -0.1875 to 0.1875
- factor_top: bfloat16 [512, 512], replicated, may hold values from -0.1875 to 0.1875
- diag_one: float32 [512, 512], replicated, may hold values from -2 to 4, as said below
- diag_two: float32 [512, 512], replicated, may hold values from -2 to 4, as said below
- pattern: int32 [2, 8], replicated, may hold values from 0 to 15, as said below
Outputs:
- inv_cols_one: float32 [2048, 512], P(('prow', 'pcol'))
- diag_block_one: float32 [512, 512], replicated
- inv_cols_two: float32 [2048, 512], P(('prow', 'pcol'))
- inv_top_two: float32 [512, 512], replicated
- diag_block_two: float32 [512, 512], replicated
The draws below stay inside these ranges and needn't reach their ends.
Inputs may be any that keep to these rules, and one draw needn't show every extreme that they name: `pattern`: each row lists 8 distinct ancestor blocks in rising order; blocks 0 and 8 are in both rows. `inverse`: Symmetric. `diag_one`: Symmetric. `diag_two`: Symmetric.
All inputs are finite; a program needn't handle non-finite values.
Results may differ from the reference program's by a relative error of at most 0.0003.
Values may be sent and summed in bfloat16 or wider, within the bound.
A program may use at most 64 MiB of HBM per device.

```python
import jax
import jax.numpy as jnp
from jax import lax

WIDTH = 512
BLOCK = 128
ANCESTORS = 2048
ANCESTOR_BLOCKS = 16
PICKED = 8


def symmetric_draw(key, order, noise_scale):
    first_key, second_key = jax.random.split(key, 2)
    shape = (order, order)
    base = jax.random.truncated_normal(first_key, -4.0, 4.0, shape, jnp.float32)
    noise = (base + base.T) * (0.7071 * noise_scale)
    diagonal = jax.random.uniform(second_key, (order,), jnp.float32, 1.0, 2.0)
    index_list = jnp.arange(order)
    return noise.at[index_list, index_list].add(diagonal)


def draw_inverse(key, part):
    return symmetric_draw(jax.random.fold_in(key, 101), ANCESTORS, 1.0)


def draw_diag_one(key, part):
    return symmetric_draw(jax.random.fold_in(key, 202), WIDTH, 1.0 / WIDTH ** 0.5)


def draw_diag_two(key, part):
    return symmetric_draw(jax.random.fold_in(key, 303), WIDTH, 1.0 / WIDTH ** 0.5)


def draw_pattern(key, part):
    chosen = []
    for which in range(2):
        region_key, score_key = jax.random.split(jax.random.fold_in(key, 411 + which))
        target_area = jax.random.randint(region_key, (), 0, 4)
        score_values = jax.random.randint(score_key, (ANCESTOR_BLOCKS,), 0, 4096)
        index_list = jnp.arange(ANCESTOR_BLOCKS, dtype=jnp.int32)
        extra_reward = jnp.where(index_list * 4 // ANCESTOR_BLOCKS == target_area, 2048, 0)
        forced = (index_list == 0) | (index_list == ANCESTOR_BLOCKS // 2)
        first_reward = jnp.where(forced, 8192, 0)
        running_totals = (score_values + extra_reward + first_reward) * ANCESTOR_BLOCKS + index_list
        ranked = jnp.argsort(-running_totals)
        chosen.append(jnp.sort(ranked[:PICKED]))
    return jnp.stack(chosen).astype(jnp.int32)


def shard_levels(key, dims, cuts, low, largest):
    level, own = 1.0, jax.random.fold_in(key, 6)
    for position, parts in cuts:
        heights = jnp.exp(jax.random.uniform(jax.random.fold_in(own, position), (parts,), jnp.float32, low / len(cuts), largest / len(cuts)))
        level = level * jnp.repeat(heights, dims[position] // parts).reshape([-1 if axis == position else 1 for axis in range(len(dims))])
    return level


def scatter_about(own_key, dims, width, limit, pieces=(), kind=jnp.bfloat16):
    values = width * jax.random.normal(own_key, dims, jnp.float32)
    if pieces:
        values = values * shard_levels(own_key, dims, pieces, -0.22, 0.18)
    return jnp.clip(values, -limit, limit).astype(kind)


def setup_inputs(seed: int = 0) -> dict:
    seeds = jax.random.split(jax.random.key(seed), 8)
    return {
        "inverse": draw_inverse(jax.random.fold_in(seeds[7], 71), 0),
        "factor_one": scatter_about(seeds[1], (ANCESTORS, WIDTH), (ANCESTORS // 2) ** -0.5, 0.1875, ((0, 16),)),
        "factor_two": scatter_about(seeds[2], (ANCESTORS, WIDTH), (ANCESTORS // 2) ** -0.5, 0.1875, ((0, 16),)),
        "factor_top": scatter_about(seeds[3], (WIDTH, WIDTH), (ANCESTORS // 2) ** -0.5, 0.1875),
        "diag_one": draw_diag_one(jax.random.fold_in(seeds[7], 71), 0),
        "diag_two": draw_diag_two(jax.random.fold_in(seeds[7], 71), 0),
        "pattern": draw_pattern(jax.random.fold_in(seeds[7], 71), 0),
    }


highest_precision = lax.Precision.HIGHEST


def pattern_rows(pattern_row):
    blocks = jnp.arange(ANCESTORS, dtype=jnp.int32) // BLOCK
    hits = blocks[:, None] == pattern_row[None, :]
    return jnp.max(hits.astype(jnp.float32), axis=1)


def product(left, right):
    return jnp.dot(left, right, precision=highest_precision, preferred_element_type=jnp.float32)


def reference(inverse, factor_one, factor_two, factor_top, diag_one, diag_two, pattern):
    mask_one = pattern_rows(pattern[0])
    second_supernode_mask = pattern_rows(pattern[1])
    lead_one = factor_one * mask_one[:, None].astype(jnp.bfloat16)
    lead_two = factor_two * second_supernode_mask[:, None].astype(jnp.bfloat16)
    inv_cols_one = -(mask_one[:, None] * product(inverse, lead_one))
    diag_block_one = diag_one - product(lead_one.astype(jnp.float32).T, inv_cols_one)
    inv_cols_two = -(second_supernode_mask[:, None] * (product(inverse, lead_two) + product(inv_cols_one, factor_top)))
    inv_top_two = -(product(inv_cols_one.T, lead_two.astype(jnp.float32)) + product(diag_block_one, factor_top))
    diag_block_two = diag_two - product(lead_two.astype(jnp.float32).T, inv_cols_two) - product(factor_top.T, inv_top_two)
    return inv_cols_one, diag_block_one, inv_cols_two, inv_top_two, diag_block_two
```

```python
import jax
import jax.numpy as jnp
from jax import lax
from jax.experimental import pallas as pl
from jax.experimental.pallas import tpu as pltpu
from jax.sharding import PartitionSpec as P

BLOCK = 128


def row_mask(pattern_row, leading_row_index, row_count):
    row_ids = leading_row_index + lax.iota(jnp.int32, row_count)
    hits = (row_ids // BLOCK)[:, None] == pattern_row[None, :]
    return jnp.max(hits.astype(jnp.float32), axis=1)


def split(x):
    high = lax.reduce_precision(x, 8, 7).astype(jnp.bfloat16)
    low = (x - high.astype(jnp.float32)).astype(jnp.bfloat16)
    return high, low


def dot(left, right, dims):
    return lax.dot_general(left, right, (dims, ((), ())), preferred_element_type=jnp.float32)


def dot_left(left, right, dims=((1,), (0,))):
    high, low = split(left)
    return dot(high, right, dims) + dot(low, right, dims)


def dot_right(left, right, dims=((1,), (0,))):
    high, low = split(right)
    return dot(left, high, dims) + dot(left, low, dims)


def finish(shares, own_mask_one, own_mask_two, sums, factor_top, diag_one, diag_two):
    width = factor_top.shape[0]
    inv_cols_one = -(own_mask_one[:, None] * shares[:, :width])
    inv_cols_two = -(own_mask_two[:, None] * (shares[:, width:] + dot_left(inv_cols_one, factor_top)))
    diag_block_one = diag_one + sums[:, :width]
    mirrored = sums[:, width : 2 * width]
    inv_top_two = mirrored - dot_left(diag_block_one, factor_top)
    diag_block_two = (
        diag_two
        + sums[:, 2 * width :]
        - dot_left(mirrored, factor_top, ((0,), (0,)))
        - dot_right(factor_top, inv_top_two, ((0,), (0,)))
    )
    return inv_cols_one, diag_block_one, inv_cols_two, inv_top_two, diag_block_two


def shards(inverse, factor_one, factor_two, factor_top, diag_one, diag_two, pattern):
    row_count, column_count = inverse.shape
    width = factor_top.shape[0]
    pcol_size = lax.axis_size("pcol")
    row_group = lax.axis_index("prow")
    column_group = lax.axis_index("pcol")
    keep_rows = row_count // pcol_size
    row_first = row_group * row_count
    own_local = column_group * keep_rows
    mask_one = row_mask(pattern[0], row_first, row_count)
    mask_two = row_mask(pattern[1], row_first, row_count)
    lead = jnp.concatenate(
        [
            factor_one * mask_one[:, None].astype(jnp.bfloat16),
            factor_two * mask_two[:, None].astype(jnp.bfloat16),
        ],
        axis=1,
    )
    own = lambda x: lax.dynamic_slice_in_dim(x, own_local, keep_rows, 0)
    leads = lax.all_gather(lead, "prow", axis=0, tiled=True)
    leads = lax.dynamic_slice_in_dim(leads, column_group * column_count, column_count, 0)
    shares = lax.psum_scatter(dot_left(inverse, leads), "pcol", scatter_dimension=0, tiled=True)
    own_lead, own_one, own_two = own(lead), own(mask_one), own(mask_two)
    first = dot_left(own_one[:, None] * shares[:, :width], own_lead, ((0,), (0,)))
    second = dot_left(shares[:, width:], own_lead[:, width:], ((0,), (0,)))
    sums = lax.psum(jnp.concatenate([first, second], axis=1), ("prow", "pcol"))
    return finish(shares, own_one, own_two, sums, factor_top, diag_one, diag_two)


MESH = pl.DeviceIdType.MESH
VMEM = pl.BlockSpec(memory_space=pltpu.VMEM)


def split_here(x):
    high = x.astype(jnp.bfloat16)
    return high, (x - high.astype(jnp.float32)).astype(jnp.bfloat16)


def exchange(
    inv_ref, lead_ref, mask_ref, y_ref, g_ref,
    leads, part_out, part_in, turned, slabs, sums_out, sums_in,
    fs_z, fs_b, fs_y, fs_c, fr_z, fr_y, fr_c,
    ps, pr, ts, tr, ss, sr, gs_z, gs_y, gs_x, gs_c, gr,
):
    p = lax.axis_index("prow")
    c = lax.axis_index("pcol")
    z, y, core = p // 4, (p // 2) % 2, p % 2
    rows = lead_ref.shape[1]
    half = rows // 2

    def at(z_, y_, core_):
        return (z_ * 2 + y_) * 2 + core_

    def remote(src, dst, send, recv, prow, pcol):
        return pltpu.make_async_remote_copy(
            src_ref=src, dst_ref=dst, send_sem=send, recv_sem=recv,
            device_id=(prow, pcol), device_id_type=MESH,
        )

    barrier = pltpu.get_barrier_semaphore()

    def greet(i, carry):
        other = lax.rem(p * 2 + c + i, 32)
        pl.semaphore_signal(barrier, inc=1, device_id=(other // 2, other % 2), device_id_type=MESH)
        return carry

    lax.fori_loop(1, 32, greet, 0)
    pl.semaphore_wait(barrier, 31)

    w = (1 - c) * z + c * (3 - z)
    step = 1 - 2 * c
    y_peer, c_peer = at(z, 1 - y, core), at(z, y, 1 - core)

    def block(s, y_, core_):
        low = (1 - c) * s + c * (1 - s)
        return at(low, y_, core_)

    def place(f, b):
        return leads.at[f, pl.ds(pl.multiple_of(b * rows, rows), rows), :]

    def fz(s, f, src):
        dst = place(f, block(s, y, core))
        return remote(src, dst, fs_z.at[s, f], fr_z.at[s, f], p + 4 * step, c)

    def fback(f):
        dst = place(f, block(1, y, core))
        return remote(lead_ref.at[f], dst, fs_b.at[f], fr_z.at[1, f], p - 4 * step, c)

    def fy(s, f, src):
        return remote(src, place(f, block(s, y, core)), fs_y.at[s, f], fr_y.at[s, f], y_peer, c)

    def fc(s, k, f, src):
        y_ = lax.rem(y + k, 2)
        return remote(src, place(f, block(s, y_, core)), fs_c.at[s, k, f], fr_c.at[s, k, f], c_peer, c)

    for s in (1, 0):
        @pl.when(w == s)
        def _(s=s):
            for f in (0, 1):
                fz(s, f, lead_ref.at[f]).start()
                fy(s, f, lead_ref.at[f]).start()
                if s == 1:
                    fback(f).start()
                fc(s, 0, f, lead_ref.at[f]).start()
            for f in (0, 1):
                leads[f, pl.ds(pl.multiple_of(block(s, y, core) * rows, rows), rows), :] = lead_ref[f]

    for s in (1, 0):
        for f in (0, 1):
            @pl.when(w != s)
            def _(s=s, f=f):
                mine = place(f, block(s, y, core))
                fz(s, f, mine).wait_recv()

                @pl.when((w == 2) | (w == s + 1))
                def _():
                    fz(s, f, mine).start()

                fy(s, f, mine).start()
                fc(s, 0, f, mine).start()

    for s in (1, 0):
        for f in (0, 1):
            theirs = place(f, block(s, 1 - y, core))
            fy(s, f, theirs).wait_recv()
            fc(s, 1, f, theirs).start()

    for s in (1, 0):
        for k in (0, 1):
            for f in (0, 1):
                fc(s, k, f, place(f, block(s, 0, core))).wait_recv()

    both = jnp.concatenate(split_here(inv_ref[...]), axis=0)
    for f in (0, 1):
        wide = dot(both, leads[f], ((1,), (0,)))
        part = wide[:rows] + wide[rows:]
        part_out[f, 0] = part[:half]
        part_out[f, 1] = part[half:]
        remote(part_out.at[f, 1 - c], part_in.at[f], ps.at[f], pr.at[f], p, 1 - c).start()
    for f in (0, 1):
        remote(part_out.at[f, 1 - c], part_in.at[f], ps.at[f], pr.at[f], p, 1 - c).wait_recv()
        y_ref[f] = part_out[f, c] + part_in[f]

    stacked = jnp.concatenate([y_ref[0] * mask_ref[:, :1], y_ref[1]], axis=0)
    turned[...] = stacked.T.reshape(16, 32, rows)
    g = p // 8
    slot = (p % 8) * 2 + c

    def column(j):
        return remote(turned.at[j], slabs.at[slot], ts.at[j], tr.at[slot], j, g)

    def send_column(i, carry):
        j = lax.rem(p + i, 16)

        @pl.when((j != p) | (g != c))
        def _():
            column(j).start()

        return carry

    lax.fori_loop(0, 16, send_column, 0)

    @pl.when(g == c)
    def _():
        slabs[slot] = turned[p]

    def take_column(q, carry):
        @pl.when((q != slot) | (g != c))
        def _():
            remote(turned.at[0], slabs.at[q], ts.at[0], tr.at[q], p, 1 - c).wait_recv()

        return carry

    lax.fori_loop(0, 16, take_column, 0)
    slab = [slabs[q] for q in range(16)]
    first = jnp.concatenate([s[:, :half] for s in slab], axis=1)
    second = jnp.concatenate([s[:, half:] for s in slab], axis=1)
    pieces = jnp.concatenate(split_here(first) + split_here(second), axis=0)
    left = dot(pieces[:64], leads[0], ((1,), (0,)))
    right = dot(pieces, leads[1], ((1,), (0,)))
    sums = jnp.concatenate(
        [left[:32] + left[32:], right[:32] + right[32:64], right[64:96] + right[96:]], axis=1
    )
    cut = sums.shape[1] // 2
    for k in (0, 1):
        for h in (0, 1):
            sums_out[k, h] = sums[16 * k : 16 * k + 16, h * cut : (h + 1) * cut]
    pair = remote(sums_out.at[1 - c], sums_in, ss, sr, p, 1 - c)
    pair.start()
    pair.wait_recv()
    me = 2 * p + c
    for h in (0, 1):
        g_ref[h, me] = sums_out[c, h] + sums_in[h]

    def chunk(z_, y_, core_, c_):
        return 2 * at(z_, y_, core_) + c_

    def gz(h, d):
        z_ = lax.rem(z + d, 4)
        return remote(g_ref.at[h, me], g_ref.at[h, me], gs_z.at[h, d - 1], gr.at[h, me], at(z_, y, core), c)

    def gy(h, o, i):
        return remote(g_ref.at[h, i], g_ref.at[h, i], gs_y.at[h, o], gr.at[h, i], y_peer, c)

    def gx(h, o, i):
        return remote(g_ref.at[h, i], g_ref.at[h, i], gs_x.at[h, o], gr.at[h, i], p, 1 - c)

    def gc(h, o, i):
        return remote(g_ref.at[h, i], g_ref.at[h, i], gs_c.at[h, o], gr.at[h, i], c_peer, c)

    for d in (1, 2, 3):
        for h in (0, 1):
            gz(h, d).start()

    def spread(d, carry):
        i = chunk(lax.rem(z + d, 4), y, core, c)
        for h in (0, 1):
            @pl.when(d > 0)
            def _(h=h):
                gy(h, 0, i).wait_recv()

            gy(h, d, i).start()
            gx(h, d, i).start()
            gc(h, d, i).start()
        return carry

    lax.fori_loop(0, 4, spread, 0)

    def relay(d, carry):
        z_ = lax.rem(z + d, 4)
        i = chunk(z_, 1 - y, core, c)
        gy(0, 0, i).wait_recv()
        gx(0, 4 + d, i).start()
        gc(0, 4 + d, i).start()
        k = chunk(z_, y, core, 1 - c)
        gx(1, 0, k).wait_recv()
        gy(1, 4 + d, k).start()
        gc(1, 4 + d, k).start()
        return carry

    lax.fori_loop(0, 4, relay, 0)

    def last(d, carry):
        z_ = lax.rem(z + d, 4)
        i = chunk(z_, y, core, 1 - c)
        gx(0, 0, i).wait_recv()
        gc(0, 8 + d, i).start()
        k = chunk(z_, 1 - y, core, c)
        gy(1, 0, k).wait_recv()
        gc(1, 8 + d, k).start()
        n = chunk(z_, 1 - y, core, 1 - c)
        gx(0, 0, n).wait_recv()
        gc(0, 12 + d, n).start()
        gy(1, 0, n).wait_recv()
        gc(1, 12 + d, n).start()
        return carry

    lax.fori_loop(0, 4, last, 0)

    def arrive(i, carry):
        n = 4 * (i // 2) + 2 * (1 - core) + i % 2
        for h in (0, 1):
            gc(h, 0, n).wait_recv()
        return carry

    lax.fori_loop(0, 16, arrive, 0)

    for s in (0, 1):
        for f in (0, 1):
            src = lead_ref.at[f]

            @pl.when((w == s) | (w == 2) | (w == s + 1))
            def _(s=s, f=f, src=src):
                fz(s, f, src).wait_send()

            fy(s, f, src).wait_send()
            for k in (0, 1):
                fc(s, k, f, src).wait_send()
    for f in (0, 1):
        @pl.when(w == 1)
        def _(f=f):
            fback(f).wait_send()

        remote(part_out.at[f, 1 - c], part_in.at[f], ps.at[f], pr.at[f], p, 1 - c).wait_send()

    def left_column(j, carry):
        @pl.when((j != p) | (g != c))
        def _():
            column(j).wait_send()

        return carry

    lax.fori_loop(0, 16, left_column, 0)
    pair.wait_send()
    for h in (0, 1):
        for d in (1, 2, 3):
            gz(h, d).wait_send()

    def left_sums(o, carry):
        for h in (0, 1):
            @pl.when(o < 8)
            def _(h=h):
                @pl.when((o < 4) | (h == 1))
                def _():
                    gy(h, o, me).wait_send()

                @pl.when((o < 4) | (h == 0))
                def _():
                    gx(h, o, me).wait_send()

            gc(h, o, me).wait_send()
        return carry

    lax.fori_loop(0, 16, left_sums, 0)


def tail_kernel(y_ref, g_ref, masks_ref, top_ref, one_ref, two_ref, c1_ref, d1_ref, c2_ref, t2_ref, d2_ref):
    width = top_ref.shape[0]
    top = top_ref[...]

    def by(left, dims=((1,), (0,))):
        high, low = split_here(left)
        return dot(high, top, dims) + dot(low, top, dims)

    c1 = -(masks_ref[0, :, :1] * y_ref[0])
    c1_ref[...] = c1
    c2_ref[...] = -(masks_ref[1, :, :1] * (y_ref[1] + by(c1)))
    cut = g_ref.shape[3]
    low = g_ref[0].reshape(width, cut)
    high = g_ref[1].reshape(width, cut)
    d1 = one_ref[...] + low[:, :width]
    d1_ref[...] = d1
    mirrored = jnp.concatenate([low[:, width:], high[:, : cut - width]], axis=1)
    t2 = mirrored - by(d1)
    t2_ref[...] = t2
    t2_high, t2_low = split_here(t2)
    top_t = top.T
    corner = dot(top_t, t2_high, ((1,), (0,))) + dot(top_t, t2_low, ((1,), (0,)))
    d2_ref[...] = two_ref[...] + high[:, cut - width :] - by(mirrored.T) - corner


def small_shards(inverse, factor_one, factor_two, factor_top, diag_one, diag_two, pattern):
    rows, columns = inverse.shape
    width = factor_top.shape[0]
    half = rows // 2
    p, c = lax.axis_index("prow"), lax.axis_index("pcol")
    masks = jnp.stack([row_mask(pattern[k], p * rows, rows) for k in (0, 1)])
    lead = jnp.stack([factor_one, factor_two]) * masks[:, :, None].astype(jnp.bfloat16)
    own = lax.dynamic_slice_in_dim(masks, c * half, half, 1)
    own = jnp.broadcast_to(own[:, :, None], (2, half, 128))
    f32, dma = jnp.float32, pltpu.SemaphoreType.DMA
    cut = 3 * width // 2
    y, g = pl.pallas_call(
        exchange,
        out_shape=(
            jax.ShapeDtypeStruct((2, half, width), f32),
            jax.ShapeDtypeStruct((2, 32, 16, cut), f32),
        ),
        in_specs=[VMEM] * 3,
        out_specs=(VMEM, VMEM),
        scratch_shapes=[
            pltpu.VMEM((2, columns, width), jnp.bfloat16),
            pltpu.VMEM((2, 2, half, width), f32),
            pltpu.VMEM((2, half, width), f32),
            pltpu.VMEM((16, 32, rows), f32),
            pltpu.VMEM((16, 32, rows), f32),
            pltpu.VMEM((2, 2, 16, cut), f32),
            pltpu.VMEM((2, 16, cut), f32),
            dma((2, 2)), dma((2,)), dma((2, 2)), dma((2, 2, 2)),
            dma((2, 2)), dma((2, 2)), dma((2, 2, 2)),
            dma((2,)), dma((2,)), dma((16,)), dma((16,)), dma, dma,
            dma((2, 3)), dma((2, 8)), dma((2, 8)), dma((2, 16)), dma((2, 32)),
        ],
        compiler_params=pltpu.CompilerParams(
            collective_id=0, has_side_effects=True, vmem_limit_bytes=48 * 2**20
        ),
    )(inverse, lead, own[0])
    square = jax.ShapeDtypeStruct((width, width), f32)
    thin = jax.ShapeDtypeStruct((half, width), f32)
    return pl.pallas_call(
        tail_kernel,
        out_shape=(thin, square, thin, square, square),
        in_specs=[VMEM] * 6,
        out_specs=(VMEM,) * 5,
        compiler_params=pltpu.CompilerParams(vmem_limit_bytes=48 * 2**20),
    )(y, g, own, factor_top, diag_one, diag_two)


def solution(mesh):
    in_specs = (P("prow", "pcol"), P("prow", None), P("prow", None), P(), P(), P(), P())
    out_specs = (P(("prow", "pcol"), None), P(), P(("prow", "pcol"), None), P(), P())
    small = mesh.shape["prow"] == 16 and mesh.shape["pcol"] == 2
    return jax.shard_map(small_shards if small else shards, mesh=mesh, in_specs=in_specs, out_specs=out_specs, check_vma=False)
```

```python
import functools

import jax
import jax.numpy as jnp
from jax import lax
from jax.experimental import pallas as pl
from jax.experimental.pallas import tpu as pltpu
from jax.sharding import PartitionSpec as P

BLOCK = 128


def row_mask(pattern_row, leading_row_index, row_count):
    row_ids = leading_row_index + lax.iota(jnp.int32, row_count)
    hits = (row_ids // BLOCK)[:, None] == pattern_row[None, :]
    return jnp.max(hits.astype(jnp.float32), axis=1)


def split(x):
    high = lax.reduce_precision(x, 8, 7).astype(jnp.bfloat16)
    low = (x - high.astype(jnp.float32)).astype(jnp.bfloat16)
    return high, low


def dot(left, right, dims):
    return lax.dot_general(left, right, (dims, ((), ())), preferred_element_type=jnp.float32)


def dot_left(left, right, dims=((1,), (0,))):
    high, low = split(left)
    return dot(high, right, dims) + dot(low, right, dims)


def dot_right(left, right, dims=((1,), (0,))):
    high, low = split(right)
    return dot(left, high, dims) + dot(left, low, dims)


def finish(shares, own_mask_one, own_mask_two, sums, factor_top, diag_one, diag_two):
    width = factor_top.shape[0]
    inv_cols_one = -(own_mask_one[:, None] * shares[:, :width])
    inv_cols_two = -(own_mask_two[:, None] * (shares[:, width:] + dot_left(inv_cols_one, factor_top)))
    diag_block_one = diag_one + sums[:, :width]
    mirrored = sums[:, width : 2 * width]
    inv_top_two = mirrored - dot_left(diag_block_one, factor_top)
    diag_block_two = (
        diag_two
        + sums[:, 2 * width :]
        - dot_left(mirrored, factor_top, ((0,), (0,)))
        - dot_right(factor_top, inv_top_two, ((0,), (0,)))
    )
    return inv_cols_one, diag_block_one, inv_cols_two, inv_top_two, diag_block_two


def shards(inverse, factor_one, factor_two, factor_top, diag_one, diag_two, pattern):
    row_count, column_count = inverse.shape
    width = factor_top.shape[0]
    pcol_size = lax.axis_size("pcol")
    row_group = lax.axis_index("prow")
    column_group = lax.axis_index("pcol")
    keep_rows = row_count // pcol_size
    row_first = row_group * row_count
    own_local = column_group * keep_rows
    mask_one = row_mask(pattern[0], row_first, row_count)
    mask_two = row_mask(pattern[1], row_first, row_count)
    lead = jnp.concatenate(
        [
            factor_one * mask_one[:, None].astype(jnp.bfloat16),
            factor_two * mask_two[:, None].astype(jnp.bfloat16),
        ],
        axis=1,
    )
    own = lambda x: lax.dynamic_slice_in_dim(x, own_local, keep_rows, 0)
    leads = lax.all_gather(lead, "prow", axis=0, tiled=True)
    leads = lax.dynamic_slice_in_dim(leads, column_group * column_count, column_count, 0)
    shares = lax.psum_scatter(dot_left(inverse, leads), "pcol", scatter_dimension=0, tiled=True)
    own_lead, own_one, own_two = own(lead), own(mask_one), own(mask_two)
    first = dot_left(own_one[:, None] * shares[:, :width], own_lead, ((0,), (0,)))
    second = dot_left(shares[:, width:], own_lead[:, width:], ((0,), (0,)))
    sums = lax.psum(jnp.concatenate([first, second], axis=1), ("prow", "pcol"))
    return finish(shares, own_one, own_two, sums, factor_top, diag_one, diag_two)


LEVEL = 1.0 / 16
TOP_CODE = 32000.0
MESH = pl.DeviceIdType.MESH
HBM = pl.BlockSpec(memory_space=pltpu.HBM)
VMEM = pl.BlockSpec(memory_space=pltpu.VMEM)


def split_here(x):
    high = x.astype(jnp.bfloat16)
    return high, (x - high.astype(jnp.float32)).astype(jnp.bfloat16)


def step_size(level):
    return jnp.exp(level * LEVEL)


def encode(x):
    largest = jnp.maximum(jnp.max(jnp.abs(x), axis=1, keepdims=True), 1e-30)
    level = jnp.ceil(jnp.log(largest) * (1.0 / LEVEL)) + 1.0
    codes = jnp.round(x * (TOP_CODE / step_size(level)))
    levels = jnp.broadcast_to(level, (x.shape[0], 128))
    return jnp.concatenate([codes, levels], axis=1).astype(jnp.int32).astype(jnp.int16)


def decode(q):
    x = q.astype(jnp.float32)
    cut = x.shape[1] - 128
    return x[:, :cut] * (step_size(x[:, cut : cut + 1]) * (1.0 / TOP_CODE))


def picked(pattern_ref, which, block):
    hits = [jnp.where(pattern_ref[which, i] == block, 1.0, 0.0) for i in range(pattern_ref.shape[1])]
    return functools.reduce(jnp.maximum, hits)


def exchange(
    inv_ref, one_hbm, two_hbm, pattern_hbm,
    y_ref, g_ref, mask_ref,
    one_ref, two_ref, pattern_ref, load_sem,
    lead_ref, inv, inv_sem, leads, part_out, part_in, turned, slabs, sums_out, sums_in,
    fs_z, fs_b, fs_y, fs_c, fr_z, fr_y, fr_c,
    ps, pr, ts, tr, ss, sr, gs_z, gs, gs_c, gr_z, gr, gr_c,
):
    p = lax.axis_index("prow")
    c = lax.axis_index("pcol")
    z, y, core = p // 4, (p // 2) % 2, p % 2
    rows = lead_ref.shape[1]
    half = rows // 2
    loads = [
        pltpu.make_async_copy(src, dst, load_sem.at[i])
        for i, (src, dst) in enumerate([
            (pattern_hbm, pattern_ref), (one_hbm, one_ref), (two_hbm, two_ref),
        ])
    ]
    fetch = pltpu.make_async_copy(inv_ref, inv, inv_sem)
    for load in loads:
        load.start()
    fetch.start()

    def at(z_, y_, core_):
        return (z_ * 2 + y_) * 2 + core_

    def remote(src, dst, send, recv, prow, pcol):
        return pltpu.make_async_remote_copy(
            src_ref=src, dst_ref=dst, send_sem=send, recv_sem=recv,
            device_id=(prow, pcol), device_id_type=MESH,
        )

    barrier = pltpu.get_barrier_semaphore()

    def greet(i, carry):
        other = lax.rem(p * 2 + c + i, 32)
        pl.semaphore_signal(barrier, inc=1, device_id=(other // 2, other % 2), device_id_type=MESH)
        return carry

    lax.fori_loop(1, 32, greet, 0)
    for load in loads:
        load.wait()
    mask_one = picked(pattern_ref, 0, p)
    mask_ref[...] = jnp.full(mask_ref.shape, picked(pattern_ref, 1, p), jnp.float32)
    lead_ref[0] = (one_ref[...].astype(jnp.float32) * mask_one).astype(jnp.bfloat16)
    lead_ref[1] = (two_ref[...].astype(jnp.float32) * picked(pattern_ref, 1, p)).astype(jnp.bfloat16)
    pl.semaphore_wait(barrier, 31)

    w = (1 - c) * z + c * (3 - z)
    step = 1 - 2 * c
    y_peer, c_peer = at(z, 1 - y, core), at(z, y, 1 - core)

    def block(s, y_, core_):
        low = (1 - c) * s + c * (1 - s)
        return at(low, y_, core_)

    def place(f, b):
        return leads.at[f, pl.ds(pl.multiple_of(b * rows, rows), rows), :]

    def fz(s, f, src):
        dst = place(f, block(s, y, core))
        return remote(src, dst, fs_z.at[s, f], fr_z.at[s, f], p + 4 * step, c)

    def fback(f):
        dst = place(f, block(1, y, core))
        return remote(lead_ref.at[f], dst, fs_b.at[f], fr_z.at[1, f], p - 4 * step, c)

    def fy(s, f, src):
        return remote(src, place(f, block(s, y, core)), fs_y.at[s, f], fr_y.at[s, f], y_peer, c)

    def fc(s, k, f, src):
        y_ = lax.rem(y + k, 2)
        return remote(src, place(f, block(s, y_, core)), fs_c.at[s, k, f], fr_c.at[s, k, f], c_peer, c)

    for s in (1, 0):
        @pl.when(w == s)
        def _(s=s):
            for f in (0, 1):
                fz(s, f, lead_ref.at[f]).start()
                fy(s, f, lead_ref.at[f]).start()
                if s == 1:
                    fback(f).start()
                fc(s, 0, f, lead_ref.at[f]).start()
            for f in (0, 1):
                leads[f, pl.ds(pl.multiple_of(block(s, y, core) * rows, rows), rows), :] = lead_ref[f]

    def along_z(f):
        for s in (1, 0):
            @pl.when(w != s)
            def _(s=s):
                mine = place(f, block(s, y, core))
                fz(s, f, mine).wait_recv()

                @pl.when((w == 2) | (w == s + 1))
                def _():
                    fz(s, f, mine).start()

                fy(s, f, mine).start()
                fc(s, 0, f, mine).start()

    def from_y(f):
        for s in (1, 0):
            theirs = place(f, block(s, 1 - y, core))
            fy(s, f, theirs).wait_recv()
            fc(s, 1, f, theirs).start()

    def multiply(f):
        for s in (1, 0):
            for k in (0, 1):
                fc(s, k, f, place(f, block(s, 0, core))).wait_recv()
        wide = dot(both, leads[f], ((1,), (0,)))
        part = wide[:rows] + wide[rows:]
        part_out[f, 0] = part[:half]
        part_out[f, 1] = part[half:]
        remote(part_out.at[f, 1 - c], part_in.at[f], ps.at[f], pr.at[f], p, 1 - c).start()

    along_z(0)
    from_y(0)
    along_z(1)
    fetch.wait()
    both = jnp.concatenate(split_here(inv[...]), axis=0)
    multiply(0)
    from_y(1)
    multiply(1)
    for f in (0, 1):
        remote(part_out.at[f, 1 - c], part_in.at[f], ps.at[f], pr.at[f], p, 1 - c).wait_recv()
        y_ref[f] = part_out[f, c] + part_in[f]

    y_ref[0] = y_ref[0] * mask_one
    stacked = jnp.concatenate([y_ref[0], y_ref[1]], axis=0)
    turned[...] = stacked.T.reshape(16, 32, rows)
    g = p // 8
    slot = (p % 8) * 2 + c

    def column(j):
        return remote(turned.at[j], slabs.at[slot], ts.at[j], tr.at[slot], j, g)

    def send_column(i, carry):
        j = lax.rem(p + i, 16)

        @pl.when((j != p) | (g != c))
        def _():
            column(j).start()

        return carry

    lax.fori_loop(0, 16, send_column, 0)

    @pl.when(g == c)
    def _():
        slabs[slot] = turned[p]

    def take_column(q, carry):
        @pl.when((q != slot) | (g != c))
        def _():
            remote(turned.at[0], slabs.at[q], ts.at[0], tr.at[q], p, 1 - c).wait_recv()

        return carry

    lax.fori_loop(0, 16, take_column, 0)
    slab = [slabs[q] for q in range(16)]
    first = jnp.concatenate([s[:, :half] for s in slab], axis=1)
    second = jnp.concatenate([s[:, half:] for s in slab], axis=1)
    pieces = jnp.concatenate(split_here(first) + split_here(second), axis=0)
    left = dot(pieces[:64], leads[0], ((1,), (0,)))
    right = dot(pieces, leads[1], ((1,), (0,)))
    sums = jnp.concatenate(
        [left[:32] + left[32:], right[:32] + right[32:64], right[64:96] + right[96:]], axis=1
    )
    cut = sums.shape[1] // 2
    for k in (0, 1):
        for h in (0, 1):
            sums_out[k, h] = sums[16 * k : 16 * k + 16, h * cut : (h + 1) * cut]
    pair = remote(sums_out.at[1 - c], sums_in, ss, sr, p, 1 - c)
    pair.start()
    pair.wait_recv()
    def line(core_, c_, y_):
        return ((core_ * 2 + c_) * 2 + y_) * 4

    me = line(core, c, y) + z
    for h in (0, 1):
        g_ref[h, me] = encode(sums_out[c, h] + sums_in[h])

    def gz(h, d):
        z_ = lax.rem(z + d, 4)
        return remote(g_ref.at[h, me], g_ref.at[h, me], gs_z.at[h, d - 1], gr_z.at[h, z], at(z_, y, core), c)

    def run(h, c_, y_):
        return g_ref.at[h, pl.ds(line(core, c_, y_), 4)]

    def hop(h, o, c_, y_):
        src = run(h, c_, y_)
        by_y = h == (o + 1) // 2 % 2
        to = (y_peer, c) if by_y else (p, 1 - c)
        return remote(src, src, gs.at[h, o], gr.at[h, o], to[0], to[1])

    def gc(h, k):
        src = run(h, lax.rem(c + k // 2, 2), lax.rem(y + k % 2, 2))
        return remote(src, src, gs_c.at[h, k], gr_c.at[h, k], c_peer, c)

    def relayed(h):
        return (c, 1 - y) if h == 0 else (1 - c, y)

    def second(h):
        return (1 - c, y) if h == 0 else (c, 1 - y)

    for d in (1, 2, 3):
        for h in (0, 1):
            gz(h, d).start()
    for h in (0, 1):
        for d in (1, 2, 3):
            z_ = lax.rem(z + d, 4)
            from_z = g_ref.at[h, line(core, c, y) + z_]
            remote(from_z, from_z, gs_z.at[h, 0], gr_z.at[h, z_], c_peer, c).wait_recv()
        hop(h, 0, c, y).start()
        hop(h, 1, c, y).start()
        gc(h, 0).start()
    for h in (0, 1):
        hop(h, 0, *relayed(h)).wait_recv()
        hop(h, 2, *relayed(h)).start()
        gc(h, 1 + h).start()
    for h in (0, 1):
        hop(h, 1, *second(h)).wait_recv()
        gc(h, 2 - h).start()
    for h in (0, 1):
        hop(h, 2, 1 - c, 1 - y).wait_recv()
        gc(h, 3).start()
    for h in (0, 1):
        for k in range(4):
            gc(h, k).wait_recv()

    for s in (0, 1):
        for f in (0, 1):
            src = lead_ref.at[f]

            @pl.when((w == s) | (w == 2) | (w == s + 1))
            def _(s=s, f=f, src=src):
                fz(s, f, src).wait_send()

            fy(s, f, src).wait_send()
            for k in (0, 1):
                fc(s, k, f, src).wait_send()
    for f in (0, 1):
        @pl.when(w == 1)
        def _(f=f):
            fback(f).wait_send()

        remote(part_out.at[f, 1 - c], part_in.at[f], ps.at[f], pr.at[f], p, 1 - c).wait_send()

    def left_column(j, carry):
        @pl.when((j != p) | (g != c))
        def _():
            column(j).wait_send()

        return carry

    lax.fori_loop(0, 16, left_column, 0)
    pair.wait_send()
    for h in (0, 1):
        for d in (1, 2, 3):
            gz(h, d).wait_send()
        for o in range(3):
            hop(h, o, c, y).wait_send()
        for k in range(4):
            gc(h, k).wait_send()


def tail_kernel(
    y_hbm, mask_hbm, top_hbm, one_hbm, g_hbm, two_hbm, c1_ref, d1_ref, c2_ref, t2_ref, d2_ref,
    y_ref, mask_ref, top_ref, one_ref, g_ref, two_ref, sem,
):
    pairs = [
        (y_hbm, y_ref), (mask_hbm, mask_ref), (top_hbm, top_ref),
        (g_hbm, g_ref), (one_hbm, one_ref), (two_hbm, two_ref),
    ]
    loads = [pltpu.make_async_copy(src, dst, sem.at[i]) for i, (src, dst) in enumerate(pairs)]
    for load in loads:
        load.start()
    for load in loads[:3]:
        load.wait()
    width = top_ref.shape[0]
    top = top_ref[...]

    def by(left, dims=((1,), (0,))):
        high, low = split_here(left)
        return dot(high, top, dims) + dot(low, top, dims)

    c1 = -y_ref[0]
    c1_ref[...] = c1
    c2_ref[...] = -(mask_ref[:1, :1] * (y_ref[1] + by(c1)))
    for load in loads[3:]:
        load.wait()
    cut = g_ref.shape[3] - 128
    order = [((core * 2 + c) * 2 + y) * 4 + z for z in range(4) for y in (0, 1) for core in (0, 1) for c in (0, 1)]
    low = decode(jnp.concatenate([g_ref[0, i] for i in order], axis=0))
    high = decode(jnp.concatenate([g_ref[1, i] for i in order], axis=0))
    d1 = one_ref[...] + low[:, :width]
    d1_ref[...] = d1
    mirrored = jnp.concatenate([low[:, width:], high[:, : cut - width]], axis=1)
    t2 = mirrored - by(d1)
    t2_ref[...] = t2
    t2_high, t2_low = split_here(t2)
    top_t = top.T
    corner = dot(top_t, t2_high, ((1,), (0,))) + dot(top_t, t2_low, ((1,), (0,)))
    d2_ref[...] = two_ref[...] + high[:, cut - width :] - by(mirrored.T) - corner


def small_shards(inverse, factor_one, factor_two, factor_top, diag_one, diag_two, pattern):
    rows, columns = inverse.shape
    width = factor_top.shape[0]
    half = rows // 2
    f32, dma = jnp.float32, pltpu.SemaphoreType.DMA
    cut = 3 * width // 2
    square = jax.ShapeDtypeStruct((width, width), f32)
    y, g, mask = pl.pallas_call(
        exchange,
        out_shape=(
            jax.ShapeDtypeStruct((2, half, width), f32),
            jax.ShapeDtypeStruct((2, 32, 16, cut + 128), jnp.int16),
            jax.ShapeDtypeStruct((8, 128), f32),
        ),
        in_specs=[HBM] * 4,
        out_specs=(VMEM,) * 3,
        scratch_shapes=[
            pltpu.VMEM((rows, width), jnp.bfloat16),
            pltpu.VMEM((rows, width), jnp.bfloat16),
            pltpu.SMEM(pattern.shape, jnp.int32),
            dma((3,)),
            pltpu.VMEM((2, rows, width), jnp.bfloat16),
            pltpu.VMEM((rows, columns), f32),
            dma,
            pltpu.VMEM((2, columns, width), jnp.bfloat16),
            pltpu.VMEM((2, 2, half, width), f32),
            pltpu.VMEM((2, half, width), f32),
            pltpu.VMEM((16, 32, rows), f32),
            pltpu.VMEM((16, 32, rows), f32),
            pltpu.VMEM((2, 2, 16, cut), f32),
            pltpu.VMEM((2, 16, cut), f32),
            dma((2, 2)), dma((2,)), dma((2, 2)), dma((2, 2, 2)),
            dma((2, 2)), dma((2, 2)), dma((2, 2, 2)),
            dma((2,)), dma((2,)), dma((16,)), dma((16,)), dma, dma,
            dma((2, 3)), dma((2, 3)), dma((2, 4)), dma((2, 4)), dma((2, 3)), dma((2, 4)),
        ],
        compiler_params=pltpu.CompilerParams(
            collective_id=0, has_side_effects=True, vmem_limit_bytes=60 * 2**20
        ),
    )(inverse, factor_one, factor_two, pattern)
    thin = jax.ShapeDtypeStruct((half, width), f32)
    return pl.pallas_call(
        tail_kernel,
        out_shape=(thin, square, thin, square, square),
        in_specs=[HBM] * 6,
        scratch_shapes=[
            *[pltpu.VMEM(x.shape, x.dtype) for x in (y, mask, factor_top, diag_one, g, diag_two)],
            dma((6,)),
        ],
        out_specs=(VMEM,) * 5,
        compiler_params=pltpu.CompilerParams(vmem_limit_bytes=60 * 2**20),
    )(y, mask, factor_top, diag_one, g, diag_two)


def solution(mesh):
    in_specs = (P("prow", "pcol"), P("prow", None), P("prow", None), P(), P(), P(), P())
    out_specs = (P(("prow", "pcol"), None), P(), P(("prow", "pcol"), None), P(), P())
    small = mesh.shape["prow"] == 16 and mesh.shape["pcol"] == 2
    return jax.shard_map(small_shards if small else shards, mesh=mesh, in_specs=in_specs, out_specs=out_specs, check_vma=False)
```
